512 devices in a mesh: col: 8 (over y, z_hi), row: 64 (over z_lo, x, core).
Axes of the slice: x: 4, y: 4, z: 16 (z_hi: 2, z_lo: 8; z = z_hi * 8 + z_lo), core: 2. Of those that a mesh axis runs over, the one named last changes fastest.
Arguments:
- tokens: bfloat16 [512, 8192], P('row', 'col'), may hold values from -6 to 6
- grad_out: bfloat16 [512, 8192], P('row', 'col'), may hold values from -6 to 6
- gate_weight: bfloat16 [8192, 16384], P('col', 'row'), may hold values from -0.0625 to 0.0625
- up_weight: bfloat16 [8192, 16384], P('col', 'row'), may hold values from -0.0625 to 0.0625
- down_weight: bfloat16 [16384, 8192], P('row', 'col'), may hold values from -0.046875 to 0.046875
- gate_blocks: int32 [64, 8, 8], P('row', 'col'), may hold values from 0 to 15, as said below
- up_blocks: int32 [64, 8, 8], P('row', 'col'), may hold values from 0 to 15, as said below
- down_blocks: int32 [64, 8, 8], P('row', 'col'), may hold values from 0 to 15, as said below
- block_counts: int32 [64, 8, 3], P('row', 'col'), may hold values from 1 to 8, as said below
Outputs:
- grad_in: float32 [512, 8192], P('row', 'col')
- gate_delta: float32 [64, 8, 8, 128, 128], P('row', 'col')
- up_delta: float32 [64, 8, 8, 128, 128], P('row', 'col')
- down_delta: float32 [64, 8, 8, 128, 128], P('row', 'col')
The draws below stay inside these ranges and needn't reach their ends.
Inputs may be any that keep to these rules, and one draw needn't show every extreme that they name: `block_counts`: entry k of a device counts its trainable blocks of the gate (k = 0), up (k = 1) and down (k = 2) projection; for each projection some device has exactly 8. `gate_blocks`: A device's first block_counts[..., 0] entries are distinct block numbers in increasing order; the rest are 0. `up_blocks`: A device's first block_counts[..., 1] entries are distinct block numbers in increasing order; the rest are 0. `down_blocks`: A device's first block_counts[..., 2] entries are distinct block numbers in increasing order; the rest are 0.
All inputs are finite; a program needn't handle non-finite values.
Results may differ from the reference program's by a relative error of at most 0.0029.
Values may be sent and summed in bfloat16 or wider, within the bound.
No kernel may reach another device: no remote copies, remote signals or barrier semaphores. Data moves between devices by JAX's collectives and lax.ppermute only.
A program may use at most 64 MiB of HBM per device.

```python
import jax
import jax.numpy as jnp
from jax import lax

D = 8192
FF = 16384
BLOCK = 128
SLOTS = 8
TOKENS = 512
BLOCKS_DEV = 16
N_COL = 8
N_ROW = 64


def block_lists(key):
    key = jax.random.fold_in(key, 11)
    devices = N_ROW * N_COL
    entries = 3 * devices
    perm_keys = jax.random.split(jax.random.fold_in(key, 1), entries)
    shuffled = jax.vmap(lambda subkey: jax.random.permutation(subkey, BLOCKS_DEV))(perm_keys)[:, :SLOTS]
    draw_one = jax.random.randint(jax.random.fold_in(key, 2), (entries,), 1, SLOTS + 1)
    draw_two = jax.random.randint(jax.random.fold_in(key, 3), (entries,), 1, SLOTS + 1)
    counts = jnp.minimum(draw_one, draw_two).reshape(3, devices)
    fullest = jax.random.randint(jax.random.fold_in(key, 4), (3,), 0, devices)
    counts = jnp.where(jnp.arange(devices)[None, :] == fullest[:, None], SLOTS, counts)
    live_slot = jnp.arange(SLOTS)[None, None, :] < counts[:, :, None]
    shuffled = shuffled.reshape(3, devices, SLOTS)
    ordered = jnp.sort(jnp.where(live_slot, shuffled, BLOCKS_DEV), axis=-1)
    block_ids = jnp.where(live_slot, ordered, 0)
    return (counts, block_ids)


def draw_gate_blocks(key, part):
    counts, block_ids = block_lists(key)
    return block_ids[0].reshape(N_ROW, N_COL, SLOTS).astype(jnp.int32)


def draw_up_blocks(key, part):
    counts, block_ids = block_lists(key)
    return block_ids[1].reshape(N_ROW, N_COL, SLOTS).astype(jnp.int32)


def draw_down_blocks(key, part):
    counts, block_ids = block_lists(key)
    return block_ids[2].reshape(N_ROW, N_COL, SLOTS).astype(jnp.int32)


def draw_block_counts(key, part):
    counts, block_ids = block_lists(key)
    return counts.T.reshape(N_ROW, N_COL, 3).astype(jnp.int32)


def steps_of(rng, dims, shards, low, largest):
    gain = 1.0
    for dim, blocks in shards:
        steps = jax.random.uniform(jax.random.fold_in(jax.random.fold_in(rng, 6), dim), (blocks,), jnp.float32, low / len(shards), largest / len(shards))
        gain = gain * jnp.repeat(jnp.exp(steps), dims[dim] // blocks).reshape((-1,) + (1,) * (len(dims) - 1 - dim))
    return gain


def noise(rng, shape, scale, bound, shards=(), kind=jnp.bfloat16):
    drawn = jax.random.normal(rng, shape, jnp.float32) * scale
    if len(shards) > 0:
        drawn = steps_of(rng, shape, shards, -0.22, 0.18) * drawn
    return jnp.clip(drawn, min=-bound, max=bound).astype(kind)


def setup_inputs(seed: int = 0) -> dict:
    arg_keys = jax.random.split(jax.random.key(seed), 10)
    tokens = noise(arg_keys[0], (TOKENS, D), 1.0, 6.0, ((0, 64), (1, 8)))
    grad_out = noise(arg_keys[1], (TOKENS, D), 1.0, 6.0, ((0, 64), (1, 8)))
    gate_weight = noise(arg_keys[2], (D, FF), D ** -0.5, 0.0625, ((0, 8), (1, 64)))
    up_weight = noise(arg_keys[3], (D, FF), D ** -0.5, 0.0625, ((0, 8), (1, 64)))
    down_weight = noise(arg_keys[4], (FF, D), FF ** -0.5, 0.046875, ((0, 64), (1, 8)))
    gate_blocks = draw_gate_blocks(jax.random.fold_in(arg_keys[9], 71), 0)
    up_blocks = draw_up_blocks(jax.random.fold_in(arg_keys[9], 71), 0)
    down_blocks = draw_down_blocks(jax.random.fold_in(arg_keys[9], 71), 0)
    block_counts = draw_block_counts(jax.random.fold_in(arg_keys[9], 71), 0)
    return dict(tokens=tokens, grad_out=grad_out, gate_weight=gate_weight, up_weight=up_weight, down_weight=down_weight, gate_blocks=gate_blocks, up_blocks=up_blocks, down_blocks=down_blocks, block_counts=block_counts)


def swiglu_back(gate_sum, up_sum, hidden_grad):
    sigmoid = jax.nn.sigmoid(gate_sum)
    active = gate_sum * sigmoid
    hidden = active * up_sum
    silu_slope = sigmoid * (1.0 + gate_sum * (1.0 - sigmoid))
    gate_grad = hidden_grad * up_sum * silu_slope
    up_grad = hidden_grad * active
    return gate_grad, up_grad, hidden


def listed_tiles(left_rows, right_rows, block_ids, block_edge):
    row_count = left_rows.shape[0]
    per_row = right_rows.shape[1] // block_edge
    left_tiles = jnp.take(left_rows.reshape(row_count, -1, block_edge), block_ids // per_row, axis=1)
    right_tiles = jnp.take(right_rows.reshape(row_count, -1, block_edge), block_ids % per_row, axis=1)
    return jnp.einsum("tsa,tsb->sab", left_tiles.astype(jnp.float32), right_tiles.astype(jnp.float32),
                      precision=lax.Precision.HIGHEST)


def finish(tiles, live_count, tile_scale):
    live_slots = jnp.arange(tiles.shape[0], dtype=jnp.int32) < live_count
    return jnp.where(live_slots[:, None, None], tiles * tile_scale, jnp.zeros_like(tiles))


def reference(tokens, grad_out, gate_weight, up_weight, down_weight, gate_blocks, up_blocks, down_blocks, block_counts):
    contract = (((1,), (1,)), ((), ()))
    gate_sum = jnp.dot(tokens, gate_weight, preferred_element_type=jnp.float32)
    up_sum = jnp.dot(tokens, up_weight, preferred_element_type=jnp.float32)
    hidden_grad = lax.dot_general(grad_out, down_weight, contract, preferred_element_type=jnp.float32)
    gate_grad, up_grad, hidden = swiglu_back(gate_sum, up_sum, hidden_grad)
    gate_low = gate_grad.astype(jnp.bfloat16)
    up_low = up_grad.astype(jnp.bfloat16)
    grad_in = (lax.dot_general(gate_low, gate_weight, contract, preferred_element_type=jnp.float32)
               + lax.dot_general(up_low, up_weight, contract, preferred_element_type=jnp.float32))
    width_dev = D // N_COL
    hidden_dev = FF // N_ROW
    tile_scale = TOKENS ** -0.5
    gate_ids = gate_blocks.reshape(-1, SLOTS)
    up_ids = up_blocks.reshape(-1, SLOTS)
    down_ids = down_blocks.reshape(-1, SLOTS)
    count_rows = block_counts.reshape(-1, 3)

    def one_device(device):
        row_index = device // N_COL
        col_index = device % N_COL
        col_start = (col_index * width_dev).astype(jnp.int32)
        row_start = (row_index * hidden_dev).astype(jnp.int32)
        token_cols = lax.dynamic_slice_in_dim(tokens, col_start, width_dev, 1)
        grad_cols = lax.dynamic_slice_in_dim(grad_out, col_start, width_dev, 1)
        gate_cols = lax.dynamic_slice_in_dim(gate_grad, row_start, hidden_dev, 1)
        up_cols = lax.dynamic_slice_in_dim(up_grad, row_start, hidden_dev, 1)
        hidden_cols = lax.dynamic_slice_in_dim(hidden, row_start, hidden_dev, 1)
        counts = count_rows[device]
        gate_tiles = finish(listed_tiles(token_cols, gate_cols, gate_ids[device], BLOCK), counts[0], tile_scale)
        up_tiles = finish(listed_tiles(token_cols, up_cols, up_ids[device], BLOCK), counts[1], tile_scale)
        down_tiles = finish(listed_tiles(hidden_cols, grad_cols, down_ids[device], BLOCK), counts[2], tile_scale)
        return gate_tiles, up_tiles, down_tiles

    gate_all, up_all, down_all = lax.map(one_device, jnp.arange(N_ROW * N_COL, dtype=jnp.int32))
    shape_out = (N_ROW, N_COL, SLOTS, BLOCK, BLOCK)
    return grad_in, gate_all.reshape(shape_out), up_all.reshape(shape_out), down_all.reshape(shape_out)
```

```python
import jax
import jax.numpy as jnp
from jax import lax
from jax.experimental import pallas as pl
from jax.experimental.pallas import tpu as pltpu
from jax.sharding import PartitionSpec as P

BLOCK = 128
NZ, NX, NC = 8, 4, 2
NY, NH = 4, 2
CODE_TOP = 32000.0
PER_OCTAVE = 128.0
CODE_ROWS = 8
NT = (((1,), (1,)), ((), ()))
TN = (((0,), (0,)), ((), ()))
BF16, F32, I16, I32 = jnp.bfloat16, jnp.float32, jnp.int16, jnp.int32

Z_GROUPS = [[z * NX * NC + w for z in range(NZ)] for w in range(NX * NC)]
X_GROUPS = [[(z * NX + x) * NC + c for x in range(NX)] for z in range(NZ) for c in range(NC)]
Y_GROUPS = [[y * NH + h for y in range(NY)] for h in range(NH)]
CORE_SWAP = [(r, r ^ 1) for r in range(NZ * NX * NC)]
H_SWAP = [(c, c ^ 1) for c in range(NY * NH)]


def encode(values):
    top = jnp.max(jnp.abs(values), axis=0, keepdims=True)
    level = jnp.ceil(jnp.log2(jnp.maximum(top, 1e-30)) * PER_OCTAVE) + 1.0
    codes = jnp.round(values * (jnp.exp2(level * (-1.0 / PER_OCTAVE)) * CODE_TOP))
    rows = jnp.concatenate([codes, jnp.broadcast_to(level, (CODE_ROWS, values.shape[1]))], axis=0)
    return rows.astype(I32).astype(I16)


def decode(coded):
    rows = coded.astype(I32).astype(F32)
    count = rows.shape[0] - CODE_ROWS
    level = rows[count : count + 1]
    return rows[:count] * (jnp.exp2(level * (1.0 / PER_OCTAVE)) * (1.0 / CODE_TOP))


def project_tokens(tokens, gate_own, gate_sib, up_own, up_sib, out):
    rows = tokens[...].reshape(-1, tokens.shape[-1])
    per = tokens.shape[1]
    for k, weight in enumerate((gate_own, gate_sib, up_own, up_sib)):
        width = weight.shape[1]
        sums = jnp.dot(rows, weight[...], preferred_element_type=F32)
        for j in range(NY):
            out[j, :, k * width : (k + 1) * width] = encode(sums[j * per : (j + 1) * per])


def project_grads(grads, down_own, down_sib, out):
    rows = grads[...].reshape(-1, grads.shape[-1])
    per = grads.shape[1]
    for k, weight in enumerate((down_own, down_sib)):
        width = weight.shape[0]
        sums = lax.dot_general(rows, weight[...], NT, preferred_element_type=F32)
        for j in range(NY):
            out[j, :, k * width : (k + 1) * width] = encode(sums[j * per : (j + 1) * per])


def add_parts(parts, total, coded):
    value = decode(parts[0])
    for j in range(1, NY):
        value = value + decode(parts[j])
    total[...] = value
    coded[...] = encode(value)


def swiglu_kernel(gu_sum, gu_coded, hg_sum, hg_coded, low, hidden_low):
    half = hg_sum.shape[1]
    gate_up = gu_sum[...] + decode(gu_coded[...])
    hidden_grad = hg_sum[...] + decode(hg_coded[...])
    gate, up = gate_up[:, :half], gate_up[:, half:]
    sigmoid = 1.0 / (1.0 + jnp.exp(-gate))
    active = gate * sigmoid
    slope = sigmoid * (1.0 + gate * (1.0 - sigmoid))
    gate_grad = (hidden_grad * up * slope).astype(BF16)
    up_grad = (hidden_grad * active).astype(BF16)
    hidden = (active * up).astype(BF16)
    for j in range(NY):
        low[j, :, :half] = gate_grad
        low[j, :, half:] = up_grad
        hidden_low[j] = hidden


def input_grad(low, gate_own, gate_sib, up_own, up_sib, out):
    rows = low[...].reshape(-1, low.shape[-1])
    width = gate_own.shape[1]
    total = None
    for k, weight in enumerate((gate_own, gate_sib, up_own, up_sib)):
        part = lax.dot_general(
            rows[:, k * width : (k + 1) * width], weight[...], NT, preferred_element_type=F32
        )
        total = part if total is None else total + part
    out[...] = total.astype(BF16).reshape(out.shape)


def add_rows(parts, out):
    value = parts[0].astype(F32)
    for j in range(1, parts.shape[0]):
        value = value + parts[j].astype(F32)
    out[...] = value.astype(out.dtype)


def delta_kernel(
    gate_ids, up_ids, down_ids, counts,
    tok_own, tok_sib, grd_own, grd_sib, low_own, low_sib, hid_own, hid_sib,
    gate_out, up_out, down_out,
):
    scale = (2 * tok_own.shape[0]) ** (-0.5)
    width = low_sib.shape[1] // 2

    def tile(ref, start):
        return ref[:, pl.ds(pl.multiple_of(start, BLOCK), BLOCK)]

    def pair(left_own, left_sib, left, right_own, right_sib, right, right_sib_at):
        first = lax.dot_general(tile(left_own, left), tile(right_own, right), TN, preferred_element_type=F32)
        second = lax.dot_general(tile(left_sib, left), tile(right_sib, right_sib_at), TN, preferred_element_type=F32)
        return (first + second) * scale

    for s in range(gate_out.shape[0]):
        live = s < counts[0]

        @pl.when(live)
        def _():
            b = gate_ids[s]
            left, right = (b // 2) * BLOCK, (b % 2) * BLOCK
            gate_out[s] = pair(tok_own, tok_sib, left, low_own, low_sib, right, right)

        @pl.when(jnp.logical_not(live))
        def _():
            gate_out[s] = jnp.zeros((BLOCK, BLOCK), F32)

    for s in range(up_out.shape[0]):
        live = s < counts[1]

        @pl.when(live)
        def _():
            b = up_ids[s]
            left, right = (b // 2) * BLOCK, (b % 2) * BLOCK
            up_out[s] = pair(tok_own, tok_sib, left, low_own, low_sib, right + 2 * width, right + width)

        @pl.when(jnp.logical_not(live))
        def _():
            up_out[s] = jnp.zeros((BLOCK, BLOCK), F32)

    for s in range(down_out.shape[0]):
        live = s < counts[2]

        @pl.when(live)
        def _():
            b = down_ids[s]
            left, right = (b // 8) * BLOCK, (b % 8) * BLOCK
            down_out[s] = pair(hid_own, hid_sib, left, grd_own, grd_sib, right, right)

        @pl.when(jnp.logical_not(live))
        def _():
            down_out[s] = jnp.zeros((BLOCK, BLOCK), F32)


VMEM = pl.BlockSpec(memory_space=pltpu.VMEM)
SMEM = pl.BlockSpec(memory_space=pltpu.SMEM)


def call(kernel, outs, *args, specs=None):
    shapes = [jax.ShapeDtypeStruct(s, d) for s, d in outs]
    single = len(shapes) == 1
    return pl.pallas_call(
        kernel,
        out_shape=shapes[0] if single else shapes,
        in_specs=specs or [VMEM] * len(args),
        out_specs=VMEM if single else [VMEM] * len(shapes),
        compiler_params=pltpu.CompilerParams(vmem_limit_bytes=40 * 1024 * 1024),
    )(*args)


def spread(values, axis, groups):
    count = len(groups[0])
    return lax.all_to_all(
        jnp.broadcast_to(values[None], (count,) + values.shape), axis, 0, 0, axis_index_groups=groups
    )


def body(tokens, grad_out, gate_w, up_w, down_w, gate_blocks, up_blocks, down_blocks, block_counts):
    rows, width = tokens.shape
    hid = gate_w.shape[1]
    part = NZ * rows
    half = NX * part

    def gather(v):
        v = spread(v, "row", Z_GROUPS).reshape(part, width)
        return spread(v, "row", X_GROUPS)

    def swap(v):
        return lax.ppermute(v, "row", CORE_SWAP)

    tok, grd = gather(tokens), gather(grad_out)
    gate_s, up_s, down_s = swap(gate_w), swap(up_w), swap(down_w)

    coded = part + CODE_ROWS

    def col_sum(v):
        v = lax.all_to_all(v, "col", 0, 0, axis_index_groups=Y_GROUPS)
        total, code = call(add_parts, [((part, v.shape[2]), F32), (v.shape[1:], I16)], v)
        return total, lax.ppermute(code, "col", H_SWAP)

    gu = col_sum(call(project_tokens, [((NY, coded, 4 * hid), I16)], tok, gate_w, gate_s, up_w, up_s))
    hg = col_sum(call(project_grads, [((NY, coded, 2 * hid), I16)], grd, down_w, down_s))
    low, hidden = call(
        swiglu_kernel, [((NY, part, 4 * hid), BF16), ((NY, part, 2 * hid), BF16)], *gu, *hg
    )
    low = lax.all_to_all(low, "col", 0, 0, axis_index_groups=Y_GROUPS)
    hidden = lax.all_to_all(hidden, "col", 0, 0, axis_index_groups=Y_GROUPS)

    grad = call(input_grad, [((NX, part, width), BF16)], low, gate_w, gate_s, up_w, up_s)
    grad = lax.all_to_all(grad, "row", 0, 0, axis_index_groups=X_GROUPS)
    grad = call(add_rows, [((part, width), BF16)], grad).reshape(NZ, rows, width)
    grad = lax.all_to_all(grad, "row", 0, 0, axis_index_groups=Z_GROUPS)
    grad = call(add_rows, [((rows, width), F32)], grad)

    tok, grd = tok.reshape(half, width), grd.reshape(half, width)
    low, hidden = low.reshape(half, 4 * hid), hidden.reshape(half, 2 * hid)
    low_s = swap(jnp.concatenate([low[:, hid : 2 * hid], low[:, 3 * hid :]], axis=1))
    hidden_s = swap(hidden[:, hid:])
    tile = ((gate_blocks.shape[-1], BLOCK, BLOCK), F32)
    deltas = call(
        delta_kernel, [tile] * 3,
        gate_blocks[0, 0], up_blocks[0, 0], down_blocks[0, 0], block_counts[0, 0],
        tok, swap(tok), grd, swap(grd), low, low_s, hidden, hidden_s,
        specs=[SMEM] * 4 + [VMEM] * 8,
    )
    return (grad, *(d[None, None] for d in deltas))


def solution(mesh):
    two, three = P("row", "col"), P("row", "col", None)
    in_specs = (two, two, P("col", "row"), P("col", "row"), two, three, three, three, three)
    tiles = P("row", "col", None, None, None)
    return jax.shard_map(
        body, mesh=mesh, in_specs=in_specs, out_specs=(two, tiles, tiles, tiles), check_vma=False
    )
```

```python
import jax
import jax.numpy as jnp
from jax import lax
from jax.experimental import pallas as pl
from jax.experimental.pallas import tpu as pltpu
from jax.sharding import PartitionSpec as P

BLOCK = 128
NZ, NX, NC = 8, 4, 2
NY, NH = 4, 2
CODE_TOP = 32000.0
PER_OCTAVE = 128.0
CODE_ROWS = 8
NT = (((1,), (1,)), ((), ()))
TN = (((0,), (0,)), ((), ()))
BF16, F32, I16, I32 = jnp.bfloat16, jnp.float32, jnp.int16, jnp.int32

Z_GROUPS = [[z * NX * NC + w for z in range(NZ)] for w in range(NX * NC)]
X_GROUPS = [[(z * NX + x) * NC + c for x in range(NX)] for z in range(NZ) for c in range(NC)]
Y_GROUPS = [[y * NH + h for y in range(NY)] for h in range(NH)]
CORE_SWAP = [(r, r ^ 1) for r in range(NZ * NX * NC)]
H_GROUPS = [[y * NH + h for h in range(NH)] for y in range(NY)]


def encode(values):
    top = jnp.max(jnp.abs(values), axis=0, keepdims=True)
    level = jnp.ceil(jnp.log2(jnp.maximum(top, 1e-30)) * PER_OCTAVE) + 1.0
    codes = jnp.round(values * (jnp.exp2(level * (-1.0 / PER_OCTAVE)) * CODE_TOP))
    rows = jnp.concatenate([codes, jnp.broadcast_to(level, (CODE_ROWS, values.shape[1]))], axis=0)
    return rows.astype(I32).astype(I16)


def decode(coded):
    rows = coded.astype(I32).astype(F32)
    count = rows.shape[0] - CODE_ROWS
    level = rows[count : count + 1]
    return rows[:count] * (jnp.exp2(level * (1.0 / PER_OCTAVE)) * (1.0 / CODE_TOP))


def project(acts, gate_own, gate_sib, up_own, up_sib, down_own, down_sib, out):
    per, width = acts.shape[1], acts.shape[2] // 2
    rows = acts[...].reshape(-1, 2 * width)
    tokens, grads = rows[:, :width], rows[:, width:]
    hid = gate_own.shape[1]

    def put(k, sums):
        for j in range(NY):
            out[j, :, k * hid : (k + 1) * hid] = encode(sums[j * per : (j + 1) * per])

    put(0, jnp.dot(tokens, gate_own[...], preferred_element_type=F32))
    put(1, jnp.dot(tokens, up_own[...], preferred_element_type=F32))
    put(2, lax.dot_general(grads, down_own[...], NT, preferred_element_type=F32))
    put(3, jnp.dot(tokens, gate_sib[...], preferred_element_type=F32))
    put(4, jnp.dot(tokens, up_sib[...], preferred_element_type=F32))
    put(5, lax.dot_general(grads, down_sib[...], NT, preferred_element_type=F32))


def add_parts(parts, coded):
    value = decode(parts[0])
    for j in range(1, NY):
        value = value + decode(parts[j])
    coded[...] = encode(value)


def swiglu_kernel(coded, low):
    values = decode(coded[0]) + decode(coded[1])
    hid = values.shape[1] // (3 * NC)
    for k in range(NC):
        at = 3 * k * hid
        gate, up, hidden_grad = (values[:, at + i * hid : at + (i + 1) * hid] for i in range(3))
        sigmoid = 1.0 / (1.0 + jnp.exp(-gate))
        active = gate * sigmoid
        slope = sigmoid * (1.0 + gate * (1.0 - sigmoid))
        results = (hidden_grad * up * slope, hidden_grad * active, active * up)
        for i, result in enumerate(results):
            low[:, at + i * hid : at + (i + 1) * hid] = result.astype(BF16)


def input_grad(low, gate_own, gate_sib, up_own, up_sib, out):
    rows = low[...].reshape(-1, low.shape[-1])
    hid = gate_own.shape[1]
    total = None
    for k, weight in ((0, gate_own), (1, up_own), (3, gate_sib), (4, up_sib)):
        part = lax.dot_general(
            rows[:, k * hid : (k + 1) * hid], weight[...], NT, preferred_element_type=F32
        )
        total = part if total is None else total + part
    out[...] = total.astype(BF16).reshape(out.shape)


def add_rows(parts, out):
    value = parts[0].astype(F32)
    for j in range(1, parts.shape[0]):
        value = value + parts[j].astype(F32)
    out[...] = value.astype(out.dtype)


def delta_kernel(
    gate_ids, up_ids, down_ids, counts, act_own, act_sib, low_own, low_sib, gate_out, up_out, down_out
):
    scale = (2 * act_own.shape[0]) ** (-0.5)
    width = act_own.shape[1] // 2
    hid = low_sib.shape[1] // 3

    def tile(ref, start):
        return ref[:, pl.ds(pl.multiple_of(start, BLOCK), BLOCK)]

    def pair(own, sib, left, right_own, right_sib, right):
        first = lax.dot_general(tile(own, left), tile(right_own, right), TN, preferred_element_type=F32)
        second = lax.dot_general(tile(sib, left), tile(right_sib, right), TN, preferred_element_type=F32)
        return (first + second) * scale

    def fill(out, count, compute):
        for s in range(out.shape[0]):
            live = s < count

            @pl.when(live)
            def _():
                out[s] = compute(s)

            @pl.when(jnp.logical_not(live))
            def _():
                out[s] = jnp.zeros((BLOCK, BLOCK), F32)

    def from_tokens(ids, base):
        def compute(s):
            b = ids[s]
            per = hid // BLOCK
            return pair(act_own, act_sib, (b // per) * BLOCK, low_own, low_sib, base + (b % per) * BLOCK)

        return compute

    def from_hidden(s):
        b = down_ids[s]
        per = width // BLOCK
        left, right = 2 * hid + (b // per) * BLOCK, width + (b % per) * BLOCK
        return pair(low_own, low_sib, left, act_own, act_sib, right)

    fill(gate_out, counts[0], from_tokens(gate_ids, 0))
    fill(up_out, counts[1], from_tokens(up_ids, hid))
    fill(down_out, counts[2], from_hidden)


VMEM = pl.BlockSpec(memory_space=pltpu.VMEM)
SMEM = pl.BlockSpec(memory_space=pltpu.SMEM)


def call(kernel, outs, *args, specs=None):
    shapes = [jax.ShapeDtypeStruct(s, d) for s, d in outs]
    single = len(shapes) == 1
    return pl.pallas_call(
        kernel,
        out_shape=shapes[0] if single else shapes,
        in_specs=specs or [VMEM] * len(args),
        out_specs=VMEM if single else [VMEM] * len(shapes),
        compiler_params=pltpu.CompilerParams(vmem_limit_bytes=16 * 1024 * 1024),
    )(*args)


def spread(values, axis, groups):
    count = len(groups[0])
    return lax.all_to_all(
        jnp.broadcast_to(values[None], (count,) + values.shape), axis, 0, 0, axis_index_groups=groups
    )


def body(tokens, grad_out, gate_w, up_w, down_w, gate_blocks, up_blocks, down_blocks, block_counts):
    rows, width = tokens.shape
    hid = gate_w.shape[1]
    part = NZ * rows
    half = NX * part
    cols = 3 * NC * hid

    def swap(v):
        return lax.ppermute(v, "row", CORE_SWAP)

    acts = spread(jnp.concatenate([tokens, grad_out], axis=1), "row", Z_GROUPS).reshape(part, 2 * width)
    acts, gate_s, up_s, down_s = lax.optimization_barrier((acts, swap(gate_w), swap(up_w), swap(down_w)))
    acts = spread(acts, "row", X_GROUPS)

    coded = part + CODE_ROWS
    sums = call(project, [((NY, coded, cols), I16)], acts, gate_w, gate_s, up_w, up_s, down_w, down_s)
    sums = lax.all_to_all(sums, "col", 0, 0, axis_index_groups=Y_GROUPS)
    acts = acts.reshape(half, 2 * width)
    code = call(add_parts, [((coded, cols), I16)], sums)
    code = lax.all_gather(code, "col", axis=0, axis_index_groups=H_GROUPS)
    low = call(swiglu_kernel, [((part, cols), BF16)], code)
    low = lax.all_gather(low, "col", axis=0, axis_index_groups=Y_GROUPS)

    grad = call(input_grad, [((NX, part, width), BF16)], low, gate_w, gate_s, up_w, up_s)
    grad = lax.all_to_all(grad, "row", 0, 0, axis_index_groups=X_GROUPS)
    low = low.reshape(half, cols)
    grad, low_s, acts_s = lax.optimization_barrier((grad, swap(low[:, cols // NC :]), swap(acts)))
    grad = call(add_rows, [((part, width), BF16)], grad).reshape(NZ, rows, width)
    grad = lax.all_to_all(grad, "row", 0, 0, axis_index_groups=Z_GROUPS)
    grad = call(add_rows, [((rows, width), F32)], grad)

    tile = ((gate_blocks.shape[-1], BLOCK, BLOCK), F32)
    deltas = call(
        delta_kernel, [tile] * 3,
        gate_blocks[0, 0], up_blocks[0, 0], down_blocks[0, 0], block_counts[0, 0],
        acts, acts_s, low, low_s,
        specs=[SMEM] * 4 + [VMEM] * 4,
    )
    return (grad, *(d[None, None] for d in deltas))


def solution(mesh):
    two, three = P("row", "col"), P("row", "col", None)
    in_specs = (two, two, P("col", "row"), P("col", "row"), two, three, three, three, three)
    tiles = P("row", "col", None, None, None)
    return jax.shard_map(
        body, mesh=mesh, in_specs=in_specs, out_specs=(two, tiles, tiles, tiles), check_vma=False
    )
```

```python
import jax
import jax.numpy as jnp
from jax import lax
from jax.experimental import pallas as pl
from jax.experimental.pallas import tpu as pltpu
from jax.sharding import PartitionSpec as P

BLOCK = 128
NZ, NX, NC = 8, 4, 2
NY, NH = 4, 2
CODE_TOP = 32000.0
PER_OCTAVE = 128.0
LANES = 128
BLOCKS = 12
LEVEL_ROWS = 16
NT = (((1,), (1,)), ((), ()))
TN = (((0,), (0,)), ((), ()))
BF16, F32, I16, I32 = jnp.bfloat16, jnp.float32, jnp.int16, jnp.int32

Z_GROUPS = [[z * NX * NC + w for z in range(NZ)] for w in range(NX * NC)]
X_GROUPS = [[(z * NX + x) * NC + c for x in range(NX)] for z in range(NZ) for c in range(NC)]
Y_GROUPS = [[y * NH + h for y in range(NY)] for h in range(NH)]
CORE_SWAP = [(r, r ^ 1) for r in range(NZ * NX * NC)]
H_GROUPS = [[y * NH + h for h in range(NH)] for y in range(NY)]


def columns(values):
    return [values[:, at : at + LANES] for at in range(0, values.shape[1], LANES)]


def encode(blocks, first=0):
    row = lax.broadcasted_iota(I32, (LEVEL_ROWS, LANES), 0)
    levels = jnp.zeros((LEVEL_ROWS, LANES), F32)
    codes = []
    for g, block in enumerate(blocks):
        top = jnp.max(jnp.abs(block), axis=0, keepdims=True)
        level = jnp.ceil(jnp.log2(jnp.maximum(top, 1e-30)) * PER_OCTAVE) + 1.0
        codes.append(jnp.round(block * (jnp.exp2(level * (-1.0 / PER_OCTAVE)) * CODE_TOP)))
        levels = jnp.where(row == first + g, level, levels)
    return codes, levels


def narrow(values):
    return values.astype(I32).astype(I16)


def decode(coded):
    rows = coded.astype(I32).astype(F32)
    count = rows.shape[0] - LEVEL_ROWS
    scales = jnp.exp2(rows[count:] * (1.0 / PER_OCTAVE)) * (1.0 / CODE_TOP)
    per = count // BLOCKS
    return [rows[g * per : (g + 1) * per] * scales[g : g + 1] for g in range(BLOCKS)]


def project(acts, gate_own, gate_sib, up_own, up_sib, down_own, down_sib, out):
    per, width = acts.shape[1], acts.shape[2] // 2
    rows = acts[...].reshape(-1, 2 * width)
    tokens, grads = rows[:, :width], rows[:, width:]
    levels = [0.0] * NY

    def put(k, sums):
        for j in range(NY):
            first = k * (sums.shape[1] // LANES)
            codes, level = encode(columns(sums[j * per : (j + 1) * per]), first)
            levels[j] = levels[j] + level
            for g, code in enumerate(codes):
                out[j, (first + g) * per : (first + g + 1) * per] = narrow(code)

    put(0, jnp.dot(tokens, gate_own[...], preferred_element_type=F32))
    put(1, jnp.dot(tokens, up_own[...], preferred_element_type=F32))
    put(2, lax.dot_general(grads, down_own[...], NT, preferred_element_type=F32))
    put(3, jnp.dot(tokens, gate_sib[...], preferred_element_type=F32))
    put(4, jnp.dot(tokens, up_sib[...], preferred_element_type=F32))
    put(5, lax.dot_general(grads, down_sib[...], NT, preferred_element_type=F32))
    for j in range(NY):
        out[j, BLOCKS * per :] = narrow(levels[j])


def add_parts(parts, coded):
    values = decode(parts[0])
    for j in range(1, NY):
        values = [a + b for a, b in zip(values, decode(parts[j]))]
    codes, levels = encode(values)
    coded[...] = narrow(jnp.concatenate([*codes, levels], axis=0))


def swiglu_kernel(coded, low):
    values = [a + b for a, b in zip(decode(coded[0]), decode(coded[1]))]
    per = BLOCKS // (3 * NC)
    for g in range(BLOCKS):
        if (g // per) % 3:
            continue
        gate, up, hidden_grad = values[g], values[g + per], values[g + 2 * per]
        sigmoid = 1.0 / (1.0 + jnp.exp(-gate))
        active = gate * sigmoid
        slope = sigmoid * (1.0 + gate * (1.0 - sigmoid))
        results = (hidden_grad * up * slope, hidden_grad * active, active * up)
        for i, result in enumerate(results):
            at = (g + i * per) * LANES
            low[:, at : at + LANES] = result.astype(BF16)


def input_grad(low, gate_own, gate_sib, up_own, up_sib, out, low_away):
    rows = low[...].reshape(-1, low.shape[-1])
    low_away[...] = rows[:, low_away.shape[1] :]
    hid = gate_own.shape[1]
    total = None
    for k, weight in ((0, gate_own), (1, up_own), (3, gate_sib), (4, up_sib)):
        part = lax.dot_general(
            rows[:, k * hid : (k + 1) * hid], weight[...], NT, preferred_element_type=F32
        )
        total = part if total is None else total + part
    out[...] = total.astype(BF16).reshape(out.shape)


def add_rows(parts, out):
    value = parts[0].astype(F32)
    for j in range(1, parts.shape[0]):
        value = value + parts[j].astype(F32)
    out[...] = value.astype(out.dtype)


def delta_kernel(
    gate_ids, up_ids, down_ids, counts, act_own, act_sib, low_own, low_sib, gate_out, up_out, down_out
):
    scale = (2 * act_own.shape[0]) ** (-0.5)
    width = act_own.shape[1] // 2
    hid = low_sib.shape[1] // 3

    def tile(ref, start):
        return ref[:, pl.ds(pl.multiple_of(start, BLOCK), BLOCK)]

    def pair(own, own_at, sib, sib_at, right_own, right_own_at, right_sib, right_sib_at):
        first = lax.dot_general(
            tile(own, own_at), tile(right_own, right_own_at), TN, preferred_element_type=F32
        )
        second = lax.dot_general(
            tile(sib, sib_at), tile(right_sib, right_sib_at), TN, preferred_element_type=F32
        )
        return (first + second) * scale

    def fill(out, count, compute):
        for s in range(out.shape[0]):
            live = s < count

            @pl.when(live)
            def _():
                out[s] = compute(s)

            @pl.when(jnp.logical_not(live))
            def _():
                out[s] = jnp.zeros((BLOCK, BLOCK), F32)

    def from_tokens(ids, base):
        def compute(s):
            b = ids[s]
            per = hid // BLOCK
            left, right = (b // per) * BLOCK, base + (b % per) * BLOCK
            return pair(act_own, left, act_sib, left, low_own, right, low_sib, right)

        return compute

    def from_hidden(s):
        b = down_ids[s]
        per = width // BLOCK
        left, right = 2 * hid + (b // per) * BLOCK, width + (b % per) * BLOCK
        return pair(low_own, left, low_sib, left, act_own, right, act_sib, right)

    fill(gate_out, counts[0], from_tokens(gate_ids, 0))
    fill(up_out, counts[1], from_tokens(up_ids, hid))
    fill(down_out, counts[2], from_hidden)


VMEM = pl.BlockSpec(memory_space=pltpu.VMEM)
SMEM = pl.BlockSpec(memory_space=pltpu.SMEM)


def call(kernel, outs, *args, specs=None, in_hbm=False):
    shapes = [pltpu.HBM(s, d) if in_hbm else jax.ShapeDtypeStruct(s, d) for s, d in outs]
    single = len(shapes) == 1
    return pl.pallas_call(
        kernel,
        out_shape=shapes[0] if single else shapes,
        in_specs=specs or [VMEM] * len(args),
        out_specs=VMEM if single else [VMEM] * len(shapes),
        compiler_params=pltpu.CompilerParams(vmem_limit_bytes=16 * 1024 * 1024),
    )(*args)


def spread(values, axis, groups):
    count = len(groups[0])
    return lax.all_to_all(
        jnp.broadcast_to(values[None], (count,) + values.shape), axis, 0, 0, axis_index_groups=groups
    )


def body(tokens, grad_out, gate_w, up_w, down_w, gate_blocks, up_blocks, down_blocks, block_counts):
    rows, width = tokens.shape
    hid = gate_w.shape[1]
    part = NZ * rows
    half = NX * part
    cols = 3 * NC * hid

    def swap(v):
        return lax.ppermute(v, "row", CORE_SWAP)

    acts = spread(jnp.concatenate([tokens, grad_out], axis=1), "row", Z_GROUPS).reshape(part, 2 * width)
    acts, gate_s, up_s, down_s = lax.optimization_barrier((acts, swap(gate_w), swap(up_w), swap(down_w)))
    acts = spread(acts, "row", X_GROUPS)

    coded = BLOCKS * part + LEVEL_ROWS
    sums = call(project, [((NY, coded, LANES), I16)], acts, gate_w, gate_s, up_w, up_s, down_w, down_s, in_hbm=True)
    sums = lax.all_to_all(sums, "col", 0, 0, axis_index_groups=Y_GROUPS)
    acts = acts.reshape(half, 2 * width)
    code = call(add_parts, [((coded, LANES), I16)], sums)
    code = lax.all_gather(code, "col", axis=0, axis_index_groups=H_GROUPS)
    low = call(swiglu_kernel, [((part, cols), BF16)], code)
    low = lax.all_gather(low, "col", axis=0, axis_index_groups=Y_GROUPS)

    grad, low_away = call(
        input_grad, [((NX, part, width), BF16), ((half, cols // NC), BF16)], low, gate_w, gate_s, up_w, up_s, in_hbm=True
    )
    grad = lax.all_to_all(grad, "row", 0, 0, axis_index_groups=X_GROUPS)
    low = low.reshape(half, cols)
    grad, low_s, acts_s = lax.optimization_barrier((grad, swap(low_away), swap(acts)))
    grad = call(add_rows, [((part, width), BF16)], grad).reshape(NZ, rows, width)
    grad = lax.all_to_all(grad, "row", 0, 0, axis_index_groups=Z_GROUPS)
    grad = call(add_rows, [((rows, width), F32)], grad)

    tile = ((gate_blocks.shape[-1], BLOCK, BLOCK), F32)
    deltas = call(
        delta_kernel, [tile] * 3,
        gate_blocks[0, 0], up_blocks[0, 0], down_blocks[0, 0], block_counts[0, 0],
        acts, acts_s, low, low_s,
        specs=[SMEM] * 4 + [VMEM] * 4,
    )
    return (grad, *(d[None, None] for d in deltas))


def solution(mesh):
    two, three = P("row", "col"), P("row", "col", None)
    in_specs = (two, two, P("col", "row"), P("col", "row"), two, three, three, three, three)
    tiles = P("row", "col", None, None, None)
    return jax.shard_map(
        body, mesh=mesh, in_specs=in_specs, out_specs=(two, tiles, tiles, tiles), check_vma=False
    )
```

```python
import jax
import jax.numpy as jnp
from jax import lax
from jax.experimental import pallas as pl
from jax.experimental.pallas import tpu as pltpu
from jax.sharding import PartitionSpec as P

BLOCK = 128
NZ, NX, NC = 8, 4, 2
NY, NH = 4, 2
CODE_TOP = 32000.0
PER_OCTAVE = 128.0
LANES = 128
BLOCKS = 12
LEVEL_ROWS = 16
NT = (((1,), (1,)), ((), ()))
TN = (((0,), (0,)), ((), ()))
BF16, F32, I16, I32 = jnp.bfloat16, jnp.float32, jnp.int16, jnp.int32

Z_ORDER = (3, 4, 2, 5, 1, 6, 0, 7)
Z_GROUPS = [[z * NX * NC + w for z in Z_ORDER] for w in range(NX * NC)]
X_GROUPS = [[(z * NX + x) * NC + c for x in range(NX)] for z in range(NZ) for c in range(NC)]
Y_GROUPS = [[y * NH + h for y in range(NY)] for h in range(NH)]
CORE_SWAP = [(r, r ^ 1) for r in range(NZ * NX * NC)]
H_GROUPS = [[y * NH + h for h in range(NH)] for y in range(NY)]


def columns(values):
    return [values[:, at : at + LANES] for at in range(0, values.shape[1], LANES)]


def encode(blocks, first=0):
    row = lax.broadcasted_iota(I32, (LEVEL_ROWS, LANES), 0)
    levels = jnp.zeros((LEVEL_ROWS, LANES), F32)
    codes = []
    for g, block in enumerate(blocks):
        top = jnp.max(jnp.abs(block), axis=0, keepdims=True)
        level = jnp.ceil(jnp.log2(jnp.maximum(top, 1e-30)) * PER_OCTAVE) + 1.0
        codes.append(jnp.round(block * (jnp.exp2(level * (-1.0 / PER_OCTAVE)) * CODE_TOP)))
        levels = jnp.where(row == first + g, level, levels)
    return codes, levels


def narrow(values):
    return values.astype(I32).astype(I16)


def decode(coded):
    rows = coded.astype(I32).astype(F32)
    count = rows.shape[0] - LEVEL_ROWS
    scales = jnp.exp2(rows[count:] * (1.0 / PER_OCTAVE)) * (1.0 / CODE_TOP)
    per = count // BLOCKS
    return [rows[g * per : (g + 1) * per] * scales[g : g + 1] for g in range(BLOCKS)]


def project(acts, gate_own, gate_sib, up_own, up_sib, down_own, down_sib, out):
    per, width = acts.shape[1], acts.shape[2] // 2
    rows = acts[...].reshape(-1, 2 * width)
    tokens, grads = rows[:, :width], rows[:, width:]
    levels = [0.0] * NY

    def put(k, sums):
        for j in range(NY):
            first = k * (sums.shape[1] // LANES)
            codes, level = encode(columns(sums[j * per : (j + 1) * per]), first)
            levels[j] = levels[j] + level
            for g, code in enumerate(codes):
                out[j, (first + g) * per : (first + g + 1) * per] = narrow(code)

    put(0, jnp.dot(tokens, gate_own[...], preferred_element_type=F32))
    put(1, jnp.dot(tokens, up_own[...], preferred_element_type=F32))
    put(2, lax.dot_general(grads, down_own[...], NT, preferred_element_type=F32))
    put(3, jnp.dot(tokens, gate_sib[...], preferred_element_type=F32))
    put(4, jnp.dot(tokens, up_sib[...], preferred_element_type=F32))
    put(5, lax.dot_general(grads, down_sib[...], NT, preferred_element_type=F32))
    for j in range(NY):
        out[j, BLOCKS * per :] = narrow(levels[j])


def add_parts(parts, coded):
    values = decode(parts[0])
    for j in range(1, NY):
        values = [a + b for a, b in zip(values, decode(parts[j]))]
    codes, levels = encode(values)
    coded[...] = narrow(jnp.concatenate([*codes, levels], axis=0))


def swiglu_kernel(coded, low):
    values = [a + b for a, b in zip(decode(coded[0]), decode(coded[1]))]
    per = BLOCKS // (3 * NC)
    for g in range(BLOCKS):
        if (g // per) % 3:
            continue
        gate, up, hidden_grad = values[g], values[g + per], values[g + 2 * per]
        sigmoid = 1.0 / (1.0 + jnp.exp(-gate))
        active = gate * sigmoid
        slope = sigmoid * (1.0 + gate * (1.0 - sigmoid))
        results = (hidden_grad * up * slope, hidden_grad * active, active * up)
        for i, result in enumerate(results):
            at = (g + i * per) * LANES
            low[:, at : at + LANES] = result.astype(BF16)


def input_grad(low, gate_own, gate_sib, up_own, up_sib, out, low_away):
    rows = low[...].reshape(-1, low.shape[-1])
    low_away[...] = rows[:, low_away.shape[1] :]
    hid = gate_own.shape[1]
    total = None
    for k, weight in ((0, gate_own), (1, up_own), (3, gate_sib), (4, up_sib)):
        part = lax.dot_general(
            rows[:, k * hid : (k + 1) * hid], weight[...], NT, preferred_element_type=F32
        )
        total = part if total is None else total + part
    out[...] = total.astype(BF16).reshape(out.shape)


def add_rows(parts, out):
    value = parts[0].astype(F32)
    for j in range(1, parts.shape[0]):
        value = value + parts[j].astype(F32)
    out[...] = value.astype(out.dtype)


def delta_kernel(
    gate_ids, up_ids, down_ids, counts, act_own, act_sib, low_own, low_sib, gate_out, up_out, down_out
):
    scale = (2 * act_own.shape[0]) ** (-0.5)
    width = act_own.shape[1] // 2
    hid = low_sib.shape[1] // 3

    def tile(ref, start):
        return ref[:, pl.ds(pl.multiple_of(start, BLOCK), BLOCK)]

    def pair(own, own_at, sib, sib_at, right_own, right_own_at, right_sib, right_sib_at):
        first = lax.dot_general(
            tile(own, own_at), tile(right_own, right_own_at), TN, preferred_element_type=F32
        )
        second = lax.dot_general(
            tile(sib, sib_at), tile(right_sib, right_sib_at), TN, preferred_element_type=F32
        )
        return (first + second) * scale

    def fill(out, count, compute):
        for s in range(out.shape[0]):
            live = s < count

            @pl.when(live)
            def _():
                out[s] = compute(s)

            @pl.when(jnp.logical_not(live))
            def _():
                out[s] = jnp.zeros((BLOCK, BLOCK), F32)

    def from_tokens(ids, base):
        def compute(s):
            b = ids[s]
            per = hid // BLOCK
            left, right = (b // per) * BLOCK, base + (b % per) * BLOCK
            return pair(act_own, left, act_sib, left, low_own, right, low_sib, right)

        return compute

    def from_hidden(s):
        b = down_ids[s]
        per = width // BLOCK
        left, right = 2 * hid + (b // per) * BLOCK, width + (b % per) * BLOCK
        return pair(low_own, left, low_sib, left, act_own, right, act_sib, right)

    fill(gate_out, counts[0], from_tokens(gate_ids, 0))
    fill(up_out, counts[1], from_tokens(up_ids, hid))
    fill(down_out, counts[2], from_hidden)


VMEM = pl.BlockSpec(memory_space=pltpu.VMEM)
SMEM = pl.BlockSpec(memory_space=pltpu.SMEM)


def call(kernel, outs, *args, specs=None, in_hbm=False):
    shapes = [pltpu.HBM(s, d) if in_hbm else jax.ShapeDtypeStruct(s, d) for s, d in outs]
    single = len(shapes) == 1
    return pl.pallas_call(
        kernel,
        out_shape=shapes[0] if single else shapes,
        in_specs=specs or [VMEM] * len(args),
        out_specs=VMEM if single else [VMEM] * len(shapes),
        compiler_params=pltpu.CompilerParams(vmem_limit_bytes=16 * 1024 * 1024),
    )(*args)


def spread(values, axis, groups):
    count = len(groups[0])
    return lax.all_to_all(
        jnp.broadcast_to(values[None], (count,) + values.shape), axis, 0, 0, axis_index_groups=groups
    )


def body(tokens, grad_out, gate_w, up_w, down_w, gate_blocks, up_blocks, down_blocks, block_counts):
    rows, width = tokens.shape
    hid = gate_w.shape[1]
    part = NZ * rows
    half = NX * part
    cols = 3 * NC * hid

    def swap(v):
        return lax.ppermute(v, "row", CORE_SWAP)

    acts = spread(jnp.concatenate([tokens, grad_out], axis=1), "row", Z_GROUPS).reshape(part, 2 * width)
    acts, gate_s, up_s, down_s = lax.optimization_barrier((acts, swap(gate_w), swap(up_w), swap(down_w)))
    acts = spread(acts, "row", X_GROUPS)

    coded = BLOCKS * part + LEVEL_ROWS
    sums = call(project, [((NY, coded, LANES), I16)], acts, gate_w, gate_s, up_w, up_s, down_w, down_s, in_hbm=True)
    sums = lax.all_to_all(sums, "col", 0, 0, axis_index_groups=Y_GROUPS)
    acts = acts.reshape(half, 2 * width)
    code = call(add_parts, [((coded, LANES), I16)], sums)
    code = lax.all_gather(code, "col", axis=0, axis_index_groups=H_GROUPS)
    low = call(swiglu_kernel, [((part, cols), BF16)], code)
    low = lax.all_gather(low, "col", axis=0, axis_index_groups=Y_GROUPS)

    grad, low_away = call(
        input_grad, [((NX, part, width), BF16), ((half, cols // NC), BF16)], low, gate_w, gate_s, up_w, up_s, in_hbm=True
    )
    grad = lax.all_to_all(grad, "row", 0, 0, axis_index_groups=X_GROUPS)
    low = low.reshape(half, cols)
    grad, low_s, acts_s = lax.optimization_barrier((grad, swap(low_away), swap(acts)))
    grad = call(add_rows, [((part, width), BF16)], grad).reshape(NZ, rows, width)
    grad = lax.all_to_all(grad, "row", 0, 0, axis_index_groups=Z_GROUPS)
    grad = call(add_rows, [((rows, width), F32)], grad)

    tile = ((gate_blocks.shape[-1], BLOCK, BLOCK), F32)
    deltas = call(
        delta_kernel, [tile] * 3,
        gate_blocks[0, 0], up_blocks[0, 0], down_blocks[0, 0], block_counts[0, 0],
        acts, acts_s, low, low_s,
        specs=[SMEM] * 4 + [VMEM] * 4,
    )
    return (grad, *(d[None, None] for d in deltas))


def solution(mesh):
    two, three = P("row", "col"), P("row", "col", None)
    in_specs = (two, two, P("col", "row"), P("col", "row"), two, three, three, three, three)
    tiles = P("row", "col", None, None, None)
    return jax.shard_map(
        body, mesh=mesh, in_specs=in_specs, out_specs=(two, tiles, tiles, tiles), check_vma=False
    )
```

```python
import jax
import jax.numpy as jnp
from jax import lax
from jax.experimental import pallas as pl
from jax.experimental.pallas import tpu as pltpu
from jax.sharding import PartitionSpec as P

BLOCK = 128
NZ, NX, NC = 8, 4, 2
NY, NH = 4, 2
CODE_TOP = 32000.0
PER_OCTAVE = 128.0
LANES = 128
BLOCKS = 12
LEVEL_ROWS = 16
NT = (((1,), (1,)), ((), ()))
TN = (((0,), (0,)), ((), ()))
BF16, F32, I16, I32 = jnp.bfloat16, jnp.float32, jnp.int16, jnp.int32

Z_ORDER = (4, 3, 5, 2, 6, 1, 7, 0)
Z_GROUPS = [[z * NX * NC + w for z in Z_ORDER] for w in range(NX * NC)]
X_GROUPS = [[(z * NX + x) * NC + c for x in range(NX)] for z in range(NZ) for c in range(NC)]
Y_GROUPS = [[y * NH + h for y in range(NY)] for h in range(NH)]
CORE_SWAP = [(r, r ^ 1) for r in range(NZ * NX * NC)]
H_GROUPS = [[y * NH + h for h in range(NH)] for y in range(NY)]


def columns(values):
    return [values[:, at : at + LANES] for at in range(0, values.shape[1], LANES)]


def encode(blocks, first=0):
    row = lax.broadcasted_iota(I32, (LEVEL_ROWS, LANES), 0)
    levels = jnp.zeros((LEVEL_ROWS, LANES), F32)
    codes = []
    for g, block in enumerate(blocks):
        top = jnp.max(jnp.abs(block), axis=0, keepdims=True)
        level = jnp.ceil(jnp.log2(jnp.maximum(top, 1e-30)) * PER_OCTAVE) + 1.0
        codes.append(jnp.round(block * (jnp.exp2(level * (-1.0 / PER_OCTAVE)) * CODE_TOP)))
        levels = jnp.where(row == first + g, level, levels)
    return codes, levels


def narrow(values):
    return values.astype(I32).astype(I16)


def decode(coded):
    rows = coded.astype(I32).astype(F32)
    count = rows.shape[0] - LEVEL_ROWS
    scales = jnp.exp2(rows[count:] * (1.0 / PER_OCTAVE)) * (1.0 / CODE_TOP)
    per = count // BLOCKS
    return [rows[g * per : (g + 1) * per] * scales[g : g + 1] for g in range(BLOCKS)]


def project(acts, gate_own, gate_sib, up_own, up_sib, down_own, down_sib, out):
    per, width = acts.shape[1], acts.shape[2] // 2
    rows = acts[...].reshape(-1, 2 * width)
    tokens, grads = rows[:, :width], rows[:, width:]
    levels = [0.0] * NY

    def put(k, sums):
        for j in range(NY):
            first = k * (sums.shape[1] // LANES)
            codes, level = encode(columns(sums[j * per : (j + 1) * per]), first)
            levels[j] = levels[j] + level
            for g, code in enumerate(codes):
                out[j, (first + g) * per : (first + g + 1) * per] = narrow(code)

    put(0, jnp.dot(tokens, gate_own[...], preferred_element_type=F32))
    put(1, jnp.dot(tokens, up_own[...], preferred_element_type=F32))
    put(2, lax.dot_general(grads, down_own[...], NT, preferred_element_type=F32))
    put(3, jnp.dot(tokens, gate_sib[...], preferred_element_type=F32))
    put(4, jnp.dot(tokens, up_sib[...], preferred_element_type=F32))
    put(5, lax.dot_general(grads, down_sib[...], NT, preferred_element_type=F32))
    for j in range(NY):
        out[j, BLOCKS * per :] = narrow(levels[j])


def add_parts(parts, coded):
    values = decode(parts[0])
    for j in range(1, NY):
        values = [a + b for a, b in zip(values, decode(parts[j]))]
    codes, levels = encode(values)
    coded[...] = narrow(jnp.concatenate([*codes, levels], axis=0))


def swiglu_kernel(coded, low):
    values = [a + b for a, b in zip(decode(coded[0]), decode(coded[1]))]
    per = BLOCKS // (3 * NC)
    for g in range(BLOCKS):
        if (g // per) % 3:
            continue
        gate, up, hidden_grad = values[g], values[g + per], values[g + 2 * per]
        sigmoid = 1.0 / (1.0 + jnp.exp(-gate))
        active = gate * sigmoid
        slope = sigmoid * (1.0 + gate * (1.0 - sigmoid))
        results = (hidden_grad * up * slope, hidden_grad * active, active * up)
        for i, result in enumerate(results):
            at = (g + i * per) * LANES
            low[:, at : at + LANES] = result.astype(BF16)


def input_grad(low, gate_own, gate_sib, up_own, up_sib, out, low_away):
    rows = low[...].reshape(-1, low.shape[-1])
    low_away[...] = rows[:, low_away.shape[1] :]
    hid = gate_own.shape[1]
    total = None
    for k, weight in ((0, gate_own), (1, up_own), (3, gate_sib), (4, up_sib)):
        part = lax.dot_general(
            rows[:, k * hid : (k + 1) * hid], weight[...], NT, preferred_element_type=F32
        )
        total = part if total is None else total + part
    out[...] = total.astype(BF16).reshape(out.shape)


def add_rows(parts, out):
    value = parts[0].astype(F32)
    for j in range(1, parts.shape[0]):
        value = value + parts[j].astype(F32)
    out[...] = value.astype(out.dtype)


def delta_kernel(
    gate_ids, up_ids, down_ids, counts, act_own, act_sib, low_own, low_sib, gate_out, up_out, down_out
):
    scale = (2 * act_own.shape[0]) ** (-0.5)
    width = act_own.shape[1] // 2
    hid = low_sib.shape[1] // 3

    def tile(ref, start):
        return ref[:, pl.ds(pl.multiple_of(start, BLOCK), BLOCK)]

    def pair(own, own_at, sib, sib_at, right_own, right_own_at, right_sib, right_sib_at):
        first = lax.dot_general(
            tile(own, own_at), tile(right_own, right_own_at), TN, preferred_element_type=F32
        )
        second = lax.dot_general(
            tile(sib, sib_at), tile(right_sib, right_sib_at), TN, preferred_element_type=F32
        )
        return (first + second) * scale

    def fill(out, count, compute):
        for s in range(out.shape[0]):
            live = s < count

            @pl.when(live)
            def _():
                out[s] = compute(s)

            @pl.when(jnp.logical_not(live))
            def _():
                out[s] = jnp.zeros((BLOCK, BLOCK), F32)

    def from_tokens(ids, base):
        def compute(s):
            b = ids[s]
            per = hid // BLOCK
            left, right = (b // per) * BLOCK, base + (b % per) * BLOCK
            return pair(act_own, left, act_sib, left, low_own, right, low_sib, right)

        return compute

    def from_hidden(s):
        b = down_ids[s]
        per = width // BLOCK
        left, right = 2 * hid + (b // per) * BLOCK, width + (b % per) * BLOCK
        return pair(low_own, left, low_sib, left, act_own, right, act_sib, right)

    fill(gate_out, counts[0], from_tokens(gate_ids, 0))
    fill(up_out, counts[1], from_tokens(up_ids, hid))
    fill(down_out, counts[2], from_hidden)


VMEM = pl.BlockSpec(memory_space=pltpu.VMEM)
SMEM = pl.BlockSpec(memory_space=pltpu.SMEM)


def call(kernel, outs, *args, specs=None, in_hbm=False):
    shapes = [pltpu.HBM(s, d) if in_hbm else jax.ShapeDtypeStruct(s, d) for s, d in outs]
    single = len(shapes) == 1
    return pl.pallas_call(
        kernel,
        out_shape=shapes[0] if single else shapes,
        in_specs=specs or [VMEM] * len(args),
        out_specs=VMEM if single else [VMEM] * len(shapes),
        compiler_params=pltpu.CompilerParams(vmem_limit_bytes=16 * 1024 * 1024),
    )(*args)


def spread(values, axis, groups):
    count = len(groups[0])
    return lax.all_to_all(
        jnp.broadcast_to(values[None], (count,) + values.shape), axis, 0, 0, axis_index_groups=groups
    )


def body(tokens, grad_out, gate_w, up_w, down_w, gate_blocks, up_blocks, down_blocks, block_counts):
    rows, width = tokens.shape
    hid = gate_w.shape[1]
    part = NZ * rows
    half = NX * part
    cols = 3 * NC * hid

    def swap(v):
        return lax.ppermute(v, "row", CORE_SWAP)

    acts = spread(jnp.concatenate([tokens, grad_out], axis=1), "row", Z_GROUPS).reshape(part, 2 * width)
    acts, gate_s, up_s, down_s = lax.optimization_barrier((acts, swap(gate_w), swap(up_w), swap(down_w)))
    acts = spread(acts, "row", X_GROUPS)

    coded = BLOCKS * part + LEVEL_ROWS
    sums = call(project, [((NY, coded, LANES), I16)], acts, gate_w, gate_s, up_w, up_s, down_w, down_s, in_hbm=True)
    sums = lax.all_to_all(sums, "col", 0, 0, axis_index_groups=Y_GROUPS)
    acts = acts.reshape(half, 2 * width)
    code = call(add_parts, [((coded, LANES), I16)], sums)
    code = lax.all_gather(code, "col", axis=0, axis_index_groups=H_GROUPS)
    low = call(swiglu_kernel, [((part, cols), BF16)], code)
    low = lax.all_gather(low, "col", axis=0, axis_index_groups=Y_GROUPS)

    grad, low_away = call(
        input_grad, [((NX, part, width), BF16), ((half, cols // NC), BF16)], low, gate_w, gate_s, up_w, up_s, in_hbm=True
    )
    grad = lax.all_to_all(grad, "row", 0, 0, axis_index_groups=X_GROUPS)
    low = low.reshape(half, cols)
    grad, low_s, acts_s = lax.optimization_barrier((grad, swap(low_away), swap(acts)))
    grad = call(add_rows, [((part, width), BF16)], grad).reshape(NZ, rows, width)
    grad = lax.all_to_all(grad, "row", 0, 0, axis_index_groups=Z_GROUPS)
    grad = call(add_rows, [((rows, width), F32)], grad)

    tile = ((gate_blocks.shape[-1], BLOCK, BLOCK), F32)
    deltas = call(
        delta_kernel, [tile] * 3,
        gate_blocks[0, 0], up_blocks[0, 0], down_blocks[0, 0], block_counts[0, 0],
        acts, acts_s, low, low_s,
        specs=[SMEM] * 4 + [VMEM] * 4,
    )
    return (grad, *(d[None, None] for d in deltas))


def solution(mesh):
    two, three = P("row", "col"), P("row", "col", None)
    in_specs = (two, two, P("col", "row"), P("col", "row"), two, three, three, three, three)
    tiles = P("row", "col", None, None, None)
    return jax.shard_map(
        body, mesh=mesh, in_specs=in_specs, out_specs=(two, tiles, tiles, tiles), check_vma=False
    )
```
